1024 devices in a mesh: fsdp: 32 (over z_lo, core), rep: 32 (over x, y, z_hi).
Axes of the slice: x: 4, y: 4, z: 32 (z_hi: 2, z_lo: 16; z = z_hi * 16 + z_lo), core: 2. Of those that a mesh axis runs over, the one named last changes fastest.
Arguments:
- tokens: bfloat16 [196608, 4096], P(('fsdp', 'rep')), may hold values from -24 to 24
- frozen_base_weight: bfloat16 [4096, 512], P('fsdp'), may hold values from -8 to 8
- adapter_down_factor: bfloat16 [4096, 64], P('fsdp'), may hold values from -0.09375 to 0.09375
- adapter_up_factor: bfloat16 [64, 512], replicated, may hold values from -0.75 to 0.75
- magnitude: float32 [512], replicated, may hold values from 0.5 to 2
- output_cotangent: bfloat16 [196608, 512], P(('fsdp', 'rep')), may hold values from -8 to 8
Outputs:
- layer_out: bfloat16 [196608, 512], P(('fsdp', 'rep'))
- input_gradient: bfloat16 [196608, 4096], P(('fsdp', 'rep'))
- mag_grad: float32 [512], replicated
- up_grad: float32 [64, 512], replicated
- down_grad: float32 [4096, 64], P('fsdp')
The draws below stay inside these ranges and needn't reach their ends.
All inputs are finite; a program needn't handle non-finite values.
Results may differ from the reference program's by a relative error of at most 0.0055.
Values may be sent and summed in bfloat16 or wider, within the bound.
A program may use at most 32 MiB of HBM per device.

```python
import math
import jax
import jax.numpy as jnp
from jax import lax

INPUT_FEATURES = 4096
OUTPUT_UNITS = 512
ADAPTER_RANK = 64
TOK_DEV = 192
TOKENS = 196608
N_FSDP = 32


def draw_frozen_base_weight(key, part):
    key = jax.random.fold_in(key, 11)
    key_draw, key_rows = jax.random.split(key, 2)
    rising = 3.0 ** (jnp.arange(INPUT_FEATURES, dtype=jnp.float32) / INPUT_FEATURES)
    spread = 10.0 ** jax.random.uniform(key_rows, (INPUT_FEATURES, 1), jnp.float32)
    values = jnp.clip(jax.random.normal(key_draw, (INPUT_FEATURES, OUTPUT_UNITS), jnp.float32), -5.0, 5.0)
    return (values * rising[:, None] * spread / (6.0 * math.sqrt(INPUT_FEATURES))).astype(jnp.bfloat16)


def draw_output_cotangent(key, part):
    key = jax.random.fold_in(key, 23)
    rising = 3.0 ** (jnp.arange(TOKENS, dtype=jnp.float32) / TOKENS) / 1.7
    values = jnp.clip(jax.random.normal(key, (TOKENS, OUTPUT_UNITS), jnp.float32), -4.0, 4.0) * rising[:, None]
    return values.astype(jnp.bfloat16)


def with_spikes(result, stream_key, source, target, blocks, factor):
    def block_of(axis_at):
        return (jnp.arange(result.shape[axis_at]) // (result.shape[axis_at] // blocks)).reshape((-1,) + (1,) * (result.ndim - 1 - axis_at))

    first = jax.random.permutation(stream_key, blocks)[block_of(target)]
    far = (block_of(target) + blocks // 2) % blocks
    return jnp.where((block_of(source) == first) | (block_of(source) == far), factor * result, result)


def level_of(own_key, dims, shards, least, top_value):
    level, own = 1.0, jax.random.fold_in(own_key, 6)
    for position, blocks in shards:
        draws = jnp.exp(jax.random.uniform(jax.random.fold_in(own, position), (blocks,), jnp.float32, least / len(shards), top_value / len(shards)))
        level = level * jnp.repeat(draws, dims[position] // blocks).reshape([-1 if axis == position else 1 for axis in range(len(dims))])
    return level


def centred(own_key, shape, width, bound, cuts=(), kind=jnp.bfloat16):
    level = level_of(own_key, shape, cuts, -0.22, 0.18) if cuts else 1.0
    result = jax.random.normal(own_key, shape, jnp.float32) * width * level
    return jnp.minimum(jnp.maximum(result, -bound), bound).astype(kind)


def noise_with(key, dims, width, reach, cuts, heavy, held_as=jnp.bfloat16):
    drawn = width * jax.random.normal(key, dims, jnp.float32)
    if cuts:
        drawn = drawn * level_of(key, dims, cuts, -0.22, 0.18)
    return jnp.clip(with_spikes(drawn, jax.random.fold_in(key, 3), *heavy), -reach, reach).astype(held_as)


def setup_inputs(seed: int = 0) -> dict:
    seeds = jax.random.split(jax.random.key(seed), 7)
    tokens = noise_with(seeds[0], (TOKENS, INPUT_FEATURES), 1.0, 24.0, ((0, 1024),), (0, 1, 1024, 6.0))
    frozen_base_weight = draw_frozen_base_weight(jax.random.fold_in(seeds[6], 71), 0)
    adapter_down_factor = centred(seeds[2], (INPUT_FEATURES, ADAPTER_RANK), INPUT_FEATURES ** -0.5, 0.09375, ((0, 32),))
    adapter_up_factor = centred(seeds[3], (ADAPTER_RANK, OUTPUT_UNITS), ADAPTER_RANK ** -0.5, 0.75)
    magnitude = jnp.clip(jnp.exp(jax.random.uniform(seeds[4], (OUTPUT_UNITS,), jnp.float32, math.log(0.5), math.log(2.0))), 0.5, 2.0)
    output_cotangent = draw_output_cotangent(jax.random.fold_in(seeds[6], 71), 0)
    return dict(tokens=tokens, frozen_base_weight=frozen_base_weight, adapter_down_factor=adapter_down_factor, adapter_up_factor=adapter_up_factor, magnitude=magnitude, output_cotangent=output_cotangent)


def reference(tokens, frozen_base_weight, adapter_down_factor, adapter_up_factor, magnitude, output_cotangent):
    merged_weight = frozen_base_weight.astype(jnp.float32) + 2.0 * jnp.dot(adapter_down_factor, adapter_up_factor, preferred_element_type=jnp.float32)
    col_norm = jnp.sqrt(lax.optimization_barrier(jnp.sum(merged_weight * merged_weight, axis=0)) + 1e-06)
    scaling = magnitude / col_norm
    block_rows = TOK_DEV * N_FSDP
    number_blocks = tokens.shape[0] // block_rows
    factor = 1.0 / jnp.sqrt(jnp.float32(tokens.shape[0]))

    def one_block(totals, pieces):
        input_rows, grads_in = pieces
        low_rank_update = jnp.dot(input_rows, adapter_down_factor, preferred_element_type=jnp.float32).astype(jnp.bfloat16)
        linear_output = jnp.dot(input_rows, frozen_base_weight, preferred_element_type=jnp.float32) + 2.0 * jnp.dot(low_rank_update, adapter_up_factor, preferred_element_type=jnp.float32)
        layer_out = (linear_output * scaling).astype(jnp.bfloat16)
        scaled_output = (grads_in.astype(jnp.float32) * scaling).astype(jnp.bfloat16)
        backward_low_rank = lax.dot_general(scaled_output, adapter_up_factor, (((1,), (1,)), ((), ())), preferred_element_type=jnp.float32).astype(jnp.bfloat16)
        input_gradient = lax.dot_general(scaled_output, frozen_base_weight, (((1,), (1,)), ((), ())), preferred_element_type=jnp.float32)
        input_gradient = (input_gradient + 2.0 * lax.dot_general(backward_low_rank, adapter_down_factor, (((1,), (1,)), ((), ())), preferred_element_type=jnp.float32)).astype(jnp.bfloat16)
        mag_sum, up_sum, down_sum = totals
        mag_sum = mag_sum + lax.optimization_barrier(jnp.sum(grads_in.astype(jnp.float32) * linear_output, axis=0))
        up_sum = up_sum + 2.0 * lax.dot_general(low_rank_update, scaled_output, (((0,), (0,)), ((), ())), preferred_element_type=jnp.float32)
        down_sum = down_sum + 2.0 * lax.dot_general(input_rows, backward_low_rank, (((0,), (0,)), ((), ())), preferred_element_type=jnp.float32)
        return ((mag_sum, up_sum, down_sum), (layer_out, input_gradient))
    start = (jnp.zeros((OUTPUT_UNITS,), jnp.float32), jnp.zeros((ADAPTER_RANK, OUTPUT_UNITS), jnp.float32), jnp.zeros((INPUT_FEATURES, ADAPTER_RANK), jnp.float32))
    pieces = (tokens.reshape(number_blocks, block_rows, INPUT_FEATURES), output_cotangent.reshape(number_blocks, block_rows, OUTPUT_UNITS))
    totals, outputs = lax.scan(one_block, start, pieces)
    layer_out = outputs[0].reshape(tokens.shape[0], OUTPUT_UNITS)
    input_gradient = outputs[1].reshape(tokens.shape[0], INPUT_FEATURES)
    mag_grad = totals[0] / col_norm * factor
    up_grad = totals[1] * factor
    down_grad = totals[2] * factor
    return (layer_out, input_gradient, mag_grad, up_grad, down_grad)
```

```python
import math

import jax
import jax.numpy as jnp
from jax import lax
from jax.experimental import pallas as pl
from jax.experimental.pallas import tpu as pltpu
from jax.sharding import PartitionSpec as P

MESH = pl.DeviceIdType.MESH
F32, BF16 = jnp.float32, jnp.bfloat16
TOK, FEAT, UNITS, RANK = 192, 4096, 512, 64
NT = (((1,), (1,)), ((), ()))
TN = (((0,), (0,)), ((), ()))


class Slots:
    def __init__(self):
        self.used = 0

    def take(self, count):
        base = self.used
        self.used += count
        return base


SLOTS = Slots()
LOCAL = SLOTS.take(6)
N_CORE = SLOTS.take(1)
N_Z = SLOTS.take(16)
A_Z = SLOTS.take(16)
A_X = SLOTS.take(4)
A_CORE = SLOTS.take(1)
W_RIGHT = SLOTS.take(16)
W_LEFT = SLOTS.take(16)
W_CORE = SLOTS.take(16)
D_CORE = SLOTS.take(1)
D_X = SLOTS.take(4)
D_Y = SLOTS.take(4)
D_Q = SLOTS.take(4)
D_O = SLOTS.take(8)
D_P = SLOTS.take(16)
U_CORE = SLOTS.take(1)
U_X = SLOTS.take(4)
U_Y = SLOTS.take(4)
U_Q = SLOTS.take(4)
U_O = SLOTS.take(8)
U_P = SLOTS.take(16)
U_PC = SLOTS.take(1)
M_CORE = SLOTS.take(1)
M_P = SLOTS.take(16)
M_Q = SLOTS.take(4)
M_O = SLOTS.take(8)
OUT = SLOTS.take(18)
TOTAL = SLOTS.used

Z_OFFSETS = tuple(d for d in range(-7, 9) if d)


def device(x, y, z, c):
    x, y, z = lax.rem(x + 4, 4), lax.rem(y + 4, 4), lax.rem(z + 32, 32)
    return {"fsdp": lax.rem(z, 16) * 2 + c, "rep": (x * 4 + y) * 2 + z // 16}


def kernel(
    tok_hbm, base_hbm, down_hbm, up_hbm, mag_hbm, cot_hbm,
    lay_hbm, inp_hbm, mg_ref, ug_ref, dg_ref,
    tok, own_a, b_ref, mag, cot,
    wg, apk, ap, af,
    n_core, n_z,
    scaled_ref, back_ref, lin, lay, inp,
    d_all, d_core, d_x, d_y, d_f, d_q, d_g, d_o, d_h, d_p,
    u_all, u_core, u_e, u_x, u_f, u_y, u_g, u_q, u_h, u_o, u_p,
    m_core, m_p, m_q, m_o, m_g, m_h,
    ss, rs,
):
    f_at, r_at = lax.axis_index("fsdp"), lax.axis_index("rep")
    c, zl = lax.rem(f_at, 2), f_at // 2
    zh, xy = lax.rem(r_at, 2), r_at // 2
    x, y, z = xy // 4, lax.rem(xy, 4), zh * 16 + zl
    qb, qa = lax.rem(z, 4), z // 4
    sib = device(x, y, z, 1 - c)
    overall = 196608.0
    factor = 1.0 / math.sqrt(overall)

    def remote(src, dst, s, r, to):
        return pltpu.make_async_remote_copy(
            src_ref=src, dst_ref=dst, send_sem=ss.at[s], recv_sem=rs.at[r],
            device_id=to, device_id_type=MESH,
        )

    def arrived(dst, r):
        remote(dst, dst, r, r, sib).wait_recv()

    def left_here(src, s):
        remote(src, src, s, s, sib).wait_send()

    rows_c = pl.ds(pl.multiple_of(c * 128, 128), 128)
    loads = [
        pltpu.make_async_copy(base_hbm, wg.at[zl, rows_c], rs.at[LOCAL]),
        pltpu.make_async_copy(down_hbm, own_a, rs.at[LOCAL + 1]),
        pltpu.make_async_copy(up_hbm, b_ref, rs.at[LOCAL + 2]),
        pltpu.make_async_copy(mag_hbm, mag, rs.at[LOCAL + 3]),
        pltpu.make_async_copy(cot_hbm, cot, rs.at[LOCAL + 4]),
        pltpu.make_async_copy(tok_hbm, tok, rs.at[LOCAL + 5]),
    ]
    for load in loads:
        load.start()

    barrier = pltpu.get_barrier_semaphore()
    peers = [sib]
    peers += [device(x + i, y + j, z, c) for i in range(4) for j in range(4) if i or j]
    peers += [device(x, y, z + d, c) for d in (*range(-8, 0), *range(1, 9), 12, -12, 16)]
    for peer in peers:
        pl.semaphore_signal(barrier, 1, device_id=peer, device_id_type=MESH)

    loads[0].wait()
    loads[1].wait()
    loads[2].wait()
    w_own = wg[zl, rows_c].astype(F32)
    merged = w_own + 2.0 * jnp.dot(own_a[...], b_ref[...], preferred_element_type=F32)
    n_core[c] = jnp.sum(merged * merged, axis=0, keepdims=True)
    apk[...] = jnp.concatenate([own_a[0:64, :], own_a[64:128, :]], axis=1)
    ap[c, x, zl] = apk[pl.ds(pl.multiple_of(x * 16, 16), 16), :]
    pl.semaphore_wait(barrier, len(peers))

    right, left = device(x, y, z + 1, c), device(x, y, z - 1, c)

    n_copy = remote(n_core.at[c], n_core.at[c], N_CORE, N_CORE, sib)
    n_copy.start()

    def half(res, h):
        return wg.at[res, pl.ds(pl.multiple_of(c * 128 + h * 64, 64), 64)]

    def ring_copy(to_right, k, h):
        res = lax.rem(zl - k + 16, 16) if to_right else lax.rem(zl + k, 16)
        at = (W_RIGHT if to_right else W_LEFT) + k * 2 + h
        return remote(half(res, h), half(res, h), at, at, right if to_right else left)

    def active(to_right, k):
        if k < 7:
            return (0, 1)
        return (0,) if to_right else (1,)

    def w_core(res):
        part = wg.at[res, rows_c]
        return remote(part, part, W_CORE + res, W_CORE + res, sib)

    for h in (0, 1):
        ring_copy(True, 0, h).start()
        ring_copy(False, 0, h).start()
    w_core(zl).start()

    def a_send(i, _):
        d = i - 7

        @pl.when(d != 0)
        def _():
            remote(
                ap.at[c, x, zl], ap.at[c, x, zl], A_Z + i, A_Z + zl, device(x, y, z + d, c)
            ).start()

        return 0

    lax.fori_loop(0, 16, a_send, 0)

    n_copy.wait()
    n_z[zl] = n_core[0] + n_core[1]

    def n_send(i, _):
        d = i - 7

        @pl.when(d != 0)
        def _():
            remote(n_z.at[zl], n_z.at[zl], N_Z + i, N_Z + zl, device(x, y, z + d, c)).start()

        return 0

    lax.fori_loop(0, 16, n_send, 0)

    def ring_step(k):
        for h in (0, 1):
            for to_right in (True, False):
                if h in active(to_right, k):
                    res = lax.rem(zl - 1 - k + 16, 16) if to_right else lax.rem(zl + 1 + k, 16)
                    at = (W_RIGHT if to_right else W_LEFT) + k * 2 + h
                    arrived(half(res, h), at)
                    if k < 7 and h in active(to_right, k + 1):
                        ring_copy(to_right, k + 1, h).start()
        if k < 7:
            w_core(lax.rem(zl - 1 - k + 16, 16)).start()
            w_core(lax.rem(zl + 1 + k, 16)).start()
        else:
            w_core(lax.rem(zl + 8, 16)).start()

    ring_step(0)

    def n_wait(i, _):
        d = i - 7

        @pl.when(d != 0)
        def _():
            slot = lax.rem(zl - d + 16, 16)
            arrived(n_z.at[slot], N_Z + slot)

        return 0

    lax.fori_loop(0, 16, n_wait, 0)
    loads[3].wait()
    loads[4].wait()
    squares = jnp.sum(n_z[...], axis=0)
    col_norm = jnp.sqrt(squares + 1e-06)
    scaling = mag[...] / col_norm
    scaled = (cot[...].astype(F32) * scaling).astype(BF16)
    scaled_ref[...] = scaled
    back = lax.dot_general(scaled, b_ref[...], NT, preferred_element_type=F32).astype(BF16)
    back_ref[...] = back
    loads[5].wait()

    def columns(res):
        return pl.ds(pl.multiple_of(res * 256, 256), 256)

    def d_part(res, _):
        part = (2.0 * factor) * lax.dot_general(
            back_ref[...], tok[:, columns(res)], TN, preferred_element_type=F32
        )
        for k in range(2):
            d_all[k, :, res] = part[:, k * 128 : k * 128 + 128].reshape(4, 16, 128)
        return 0

    lax.fori_loop(0, 16, d_part, 0)
    d_core_copy = remote(d_all.at[1 - c], d_core, D_CORE, D_CORE, sib)
    d_core_copy.start()
    ring_step(1)

    def a_wait(i, _):
        d = i - 7

        @pl.when(d != 0)
        def _():
            slot = lax.rem(zl - d + 16, 16)
            arrived(ap.at[c, x, slot], A_Z + slot)

        return 0

    lax.fori_loop(0, 16, a_wait, 0)
    for d in (1, 2, 3):
        remote(ap.at[c, x], ap.at[c, x], A_X + d, A_X + d, device(x + d, y, z, c)).start()

    d_core_copy.wait()

    def d_sum(i, _):
        d_core[i] = d_core[i] + d_all[c, i]
        return 0

    lax.fori_loop(0, 4, d_sum, 0)
    for d in (1, 2, 3):
        remote(
            d_core.at[lax.rem(x + d, 4)], d_x.at[x], D_X + d, D_X + d, device(x + d, y, z, c)
        ).start()
    ring_step(2)

    for d in (1, 2, 3):
        xs = lax.rem(x - d + 4, 4)
        arrived(ap.at[c, xs], A_X + d)
    a_core_copy = remote(ap.at[c], ap.at[c], A_CORE, A_CORE, sib)
    a_core_copy.start()
    ring_step(3)
    arrived(ap.at[1 - c], A_CORE)
    for k in range(2):
        for q in range(4):
            part = ap[k, q]
            af[:, k, 0, q] = part[:, :, 0:64]
            af[:, k, 1, q] = part[:, :, 64:128]
    low = jnp.dot(tok[...], af[...].reshape(FEAT, RANK), preferred_element_type=F32).astype(BF16)
    up_part = (2.0 * factor) * lax.dot_general(low, scaled_ref[...], TN, preferred_element_type=F32)
    for k in range(2):
        for q in range(4):
            u_all[k, q] = up_part[k * 32 : k * 32 + 32, q * 128 : q * 128 + 128]
    lin[...] = 2.0 * jnp.dot(low, b_ref[...], preferred_element_type=F32)
    u_core_copy = remote(u_all.at[1 - c], u_core, U_CORE, U_CORE, sib)
    u_core_copy.start()

    d_x[x] = d_core[x]
    for d in (1, 2, 3):
        arrived(d_x.at[lax.rem(x - d + 4, 4)], D_X + d)
    d_f[...] = ((d_x[0] + d_x[1]) + (d_x[2] + d_x[3])).reshape(4, 4, 16, 128)
    for d in (1, 2, 3):
        remote(
            d_f.at[lax.rem(y + d, 4)], d_y.at[y], D_Y + d, D_Y + d, device(x, y + d, z, c)
        ).start()
    u_core_copy.wait()
    u_e[...] = u_all[c] + u_core[...]
    for d in (1, 2, 3):
        remote(
            u_e.at[lax.rem(x + d, 4)], u_x.at[x], U_X + d, U_X + d, device(x + d, y, z, c)
        ).start()
    ring_step(4)

    def consume(res):
        w_pair = wg[res]
        a_pair = af[res].reshape(256, RANK)
        lin[...] += jnp.dot(tok[:, columns(res)], w_pair, preferred_element_type=F32)
        grad = lax.dot_general(scaled_ref[...], w_pair, NT, preferred_element_type=F32)
        grad = grad + 2.0 * lax.dot_general(
            back_ref[...], a_pair, NT, preferred_element_type=F32
        )
        inp[:, columns(res)] = grad.astype(BF16)
        pltpu.make_async_copy(
            inp.at[:, columns(res)], inp_hbm.at[:, columns(res)], rs.at[OUT + res]
        ).start()

    def consume_range(first, last):
        def one(j, _):
            res = lax.rem(zl + j + (first + 16), 16)
            arrived(wg.at[res, pl.ds(pl.multiple_of((1 - c) * 128, 128), 128)], W_CORE + res)
            consume(res)
            return 0

        lax.fori_loop(0, last - first, one, 0)

    consume_range(-3, 4)

    d_y[y] = d_f[y]
    for d in (1, 2, 3):
        arrived(d_y.at[lax.rem(y - d + 4, 4)], D_Y + d)
    d_g[...] = (d_y[0] + d_y[1]) + (d_y[2] + d_y[3])
    for d in (1, 2, 3):
        to = lax.rem(qb + d, 4)
        remote(d_g.at[to], d_q.at[qb], D_Q + d, D_Q + d, device(x, y, qa * 4 + to, c)).start()
    u_x[x] = u_e[x]
    for d in (1, 2, 3):
        arrived(u_x.at[lax.rem(x - d + 4, 4)], U_X + d)
    u_f[...] = ((u_x[0] + u_x[1]) + (u_x[2] + u_x[3])).reshape(4, 8, 128)
    for d in (1, 2, 3):
        remote(
            u_f.at[lax.rem(y + d, 4)], u_y.at[y], U_Y + d, U_Y + d, device(x, y + d, z, c)
        ).start()
    ring_step(5)

    owner = lax.rem(qa, 4) == y
    d_q[qb] = d_g[qb]
    for d in (1, 2, 3):
        arrived(d_q.at[lax.rem(qb - d + 4, 4)], D_Q + d)
    d_h[...] = (d_q[0] + d_q[1]) + (d_q[2] + d_q[3])
    for hi in (0, 1):
        to = y + 4 * hi

        @pl.when(to != qa)
        def _():
            remote(d_h, d_o.at[qa], D_O + hi, D_O + qa, device(x, y, to * 4 + qb, c)).start()

    u_y[y] = u_f[y]
    for d in (1, 2, 3):
        arrived(u_y.at[lax.rem(y - d + 4, 4)], U_Y + d)
    u_q[qb] = (u_y[0] + u_y[1]) + (u_y[2] + u_y[3])
    for d in (1, 2, 3):
        to = lax.rem(qb + d, 4)
        remote(u_q.at[qb], u_q.at[qb], U_Q + d, U_Q + d, device(x, y, qa * 4 + to, c)).start()
    ring_step(6)
    for d in (1, 2, 3):
        arrived(u_q.at[lax.rem(qb - d + 4, 4)], U_Q + d)
    u_o[qa] = (u_q[0] + u_q[1]) + (u_q[2] + u_q[3])
    for d in range(1, 8):
        to = lax.rem(qa + d, 8)
        remote(u_o.at[qa], u_o.at[qa], U_O + d, U_O + d, device(x, y, to * 4 + qb, c)).start()
    ring_step(7)
    consume_range(4, 13)

    linear = lin[...]
    lay[...] = (linear * scaling).astype(BF16)
    lay_copy = pltpu.make_async_copy(lay, lay_hbm, rs.at[OUT + 16])
    lay_copy.start()
    m_core[c] = jnp.sum(cot[...].astype(F32) * linear, axis=0, keepdims=True)
    m_core_copy = remote(m_core.at[c], m_core.at[c], M_CORE, M_CORE, sib)
    m_core_copy.start()
    m_core_copy.wait()
    m_p[xy] = m_core[0] + m_core[1]

    def plane(i):
        return lax.rem(xy // 4 + i // 4, 4), lax.rem(lax.rem(xy, 4) + lax.rem(i, 4), 4)

    def m_send(i, _):
        px, py = plane(i)
        remote(m_p.at[xy], m_p.at[xy], M_P + i, M_P + xy, device(px, py, z, c)).start()
        return 0

    lax.fori_loop(1, 16, m_send, 0)

    @pl.when(owner)
    def _():
        d_o[qa] = d_h[...]
        for d in range(1, 8):
            at = lax.rem(qa - d + 8, 8)
            arrived(d_o.at[at], D_O + at)
        total = ((d_o[0] + d_o[1]) + (d_o[2] + d_o[3])) + ((d_o[4] + d_o[5]) + (d_o[6] + d_o[7]))
        d_p[x] = total

        def d_send(i, _):
            px, py = plane(i)
            remote(d_p.at[x], d_p.at[x], D_P + i, D_P + x, device(px, py, z, c)).start()
            return 0

        lax.fori_loop(1, 16, d_send, 0)

    for d in range(1, 8):
        arrived(u_o.at[lax.rem(qa - d + 8, 8)], U_O + d)
    u_p[c, xy] = ((u_o[0] + u_o[1]) + (u_o[2] + u_o[3])) + ((u_o[4] + u_o[5]) + (u_o[6] + u_o[7]))

    def u_send(i, _):
        px, py = plane(i)
        remote(u_p.at[c, xy], u_p.at[c, xy], U_P + i, U_P + xy, device(px, py, z, c)).start()
        return 0

    lax.fori_loop(1, 16, u_send, 0)

    def m_wait(i, _):
        px, py = plane(i)
        slot = px * 4 + py
        arrived(m_p.at[slot], M_P + slot)
        return 0

    lax.fori_loop(1, 16, m_wait, 0)
    m_q[qb] = jnp.sum(m_p[...], axis=0)
    for d in (1, 2, 3):
        to = lax.rem(qb + d, 4)
        remote(m_q.at[qb], m_q.at[qb], M_Q + d, M_Q + d, device(x, y, qa * 4 + to, c)).start()

    for d in (1, 2, 3):
        arrived(m_q.at[lax.rem(qb - d + 4, 4)], M_Q + d)
    m_o[qa] = (m_q[0] + m_q[1]) + (m_q[2] + m_q[3])
    for d in range(1, 8):
        to = lax.rem(qa + d, 8)
        remote(m_o.at[qa], m_o.at[qa], M_O + d, M_O + d, device(x, y, to * 4 + qb, c)).start()

    def u_wait(i, _):
        px, py = plane(i)
        slot = px * 4 + py
        arrived(u_p.at[c, slot], U_P + slot)
        return 0

    lax.fori_loop(1, 16, u_wait, 0)
    u_pc = remote(u_p.at[c], u_p.at[c], U_PC, U_PC, sib)
    u_pc.start()

    def d_wait(s, _):
        @pl.when(jnp.logical_or(s != x, jnp.logical_not(owner)))
        def _():
            arrived(d_p.at[s], D_P + s)

        return 0

    lax.fori_loop(0, 4, d_wait, 0)
    dg_ref[...] = d_p[...].reshape(64, 128).T
    arrived(u_p.at[1 - c], U_PC)
    for k in range(2):
        for q in range(4):
            ug_ref[k * 32 : k * 32 + 32, q * 128 : q * 128 + 128] = u_p[
                k, q * 4 : q * 4 + 4
            ].reshape(32, 128)
    for d in range(1, 8):
        arrived(m_o.at[lax.rem(qa - d + 8, 8)], M_O + d)
    m_sum = ((m_o[0] + m_o[1]) + (m_o[2] + m_o[3])) + ((m_o[4] + m_o[5]) + (m_o[6] + m_o[7]))
    mg_ref[...] = m_sum / col_norm * factor

    def sent_z(i, _):
        @pl.when(i != 7)
        def _():
            left_here(ap.at[c, x, zl], A_Z + i)
            left_here(n_z.at[zl], N_Z + i)

        @pl.when(i != 0)
        def _():
            left_here(m_p.at[xy], M_P + i)
            left_here(u_p.at[c, xy], U_P + i)

            @pl.when(owner)
            def _():
                left_here(d_p.at[x], D_P + i)

        left_here(wg.at[i, rows_c], W_CORE + i)
        pltpu.make_async_copy(
            inp.at[:, columns(i)], inp_hbm.at[:, columns(i)], rs.at[OUT + i]
        ).wait()
        return 0

    lax.fori_loop(0, 16, sent_z, 0)
    for k in range(8):
        for to_right in (True, False):
            for h in active(to_right, k):
                ring_copy(to_right, k, h).wait_send()
    for d in (1, 2, 3):
        left_here(ap.at[c, x], A_X + d)
        left_here(d_core.at[0], D_X + d)
        left_here(d_f.at[0], D_Y + d)
        left_here(d_g.at[0], D_Q + d)
        left_here(u_e.at[0], U_X + d)
        left_here(u_f.at[0], U_Y + d)
        left_here(u_q.at[0], U_Q + d)
        left_here(m_q.at[0], M_Q + d)
    for hi in (0, 1):

        @pl.when(y + 4 * hi != qa)
        def _():
            left_here(d_h, D_O + hi)

    for d in range(1, 8):
        left_here(u_o.at[0], U_O + d)
        left_here(m_o.at[0], M_O + d)
    left_here(ap.at[c], A_CORE)
    left_here(u_p.at[c], U_PC)
    lay_copy.wait()


def body(tokens, base, down, up, magnitude, cotangent):
    anywhere = pl.BlockSpec(memory_space=pl.ANY)
    vmem = pl.BlockSpec(memory_space=pltpu.VMEM)
    lay, inp, mg, ug, dg = pl.pallas_call(
        kernel,
        out_shape=(
            jax.ShapeDtypeStruct((TOK, UNITS), BF16),
            jax.ShapeDtypeStruct((TOK, FEAT), BF16),
            jax.ShapeDtypeStruct((1, UNITS), F32),
            jax.ShapeDtypeStruct((RANK, UNITS), F32),
            jax.ShapeDtypeStruct((128, RANK), F32),
        ),
        in_specs=[anywhere] * 6,
        out_specs=(anywhere, anywhere, vmem, vmem, vmem),
        scratch_shapes=[
            pltpu.VMEM((TOK, FEAT), BF16),
            pltpu.VMEM((128, RANK), BF16),
            pltpu.VMEM((RANK, UNITS), BF16),
            pltpu.VMEM((1, UNITS), F32),
            pltpu.VMEM((TOK, UNITS), BF16),
            pltpu.VMEM((16, 256, UNITS), BF16),
            pltpu.VMEM((64, 128), BF16),
            pltpu.VMEM((2, 4, 16, 16, 128), BF16),
            pltpu.VMEM((16, 2, 2, 4, 16, 64), BF16),
            pltpu.VMEM((2, 1, UNITS), F32),
            pltpu.VMEM((16, 1, UNITS), F32),
            pltpu.VMEM((TOK, UNITS), BF16),
            pltpu.VMEM((TOK, RANK), BF16),
            pltpu.VMEM((TOK, UNITS), F32),
            pltpu.VMEM((TOK, UNITS), BF16),
            pltpu.VMEM((TOK, FEAT), BF16),
            pltpu.VMEM((2, 4, 16, 16, 128), F32),
            pltpu.VMEM((4, 16, 16, 128), F32),
            pltpu.VMEM((4, 16, 16, 128), F32),
            pltpu.VMEM((4, 4, 16, 128), F32),
            pltpu.VMEM((4, 4, 16, 128), F32),
            pltpu.VMEM((4, 16, 128), F32),
            pltpu.VMEM((4, 16, 128), F32),
            pltpu.VMEM((8, 16, 128), F32),
            pltpu.VMEM((16, 128), F32),
            pltpu.VMEM((4, 16, 128), F32),
            pltpu.VMEM((2, 4, 32, 128), F32),
            pltpu.VMEM((4, 32, 128), F32),
            pltpu.VMEM((4, 32, 128), F32),
            pltpu.VMEM((4, 32, 128), F32),
            pltpu.VMEM((4, 8, 128), F32),
            pltpu.VMEM((4, 8, 128), F32),
            pltpu.VMEM((8, 128), F32),
            pltpu.VMEM((4, 8, 128), F32),
            pltpu.VMEM((8, 128), F32),
            pltpu.VMEM((8, 8, 128), F32),
            pltpu.VMEM((2, 16, 8, 128), F32),
            pltpu.VMEM((2, 1, UNITS), F32),
            pltpu.VMEM((16, 1, UNITS), F32),
            pltpu.VMEM((4, 1, UNITS), F32),
            pltpu.VMEM((8, 1, UNITS), F32),
            pltpu.VMEM((1, UNITS), F32),
            pltpu.VMEM((1, UNITS), F32),
            pltpu.SemaphoreType.DMA((TOTAL,)),
            pltpu.SemaphoreType.DMA((TOTAL,)),
        ],
        compiler_params=pltpu.CompilerParams(
            collective_id=0, has_side_effects=True, vmem_limit_bytes=48 * 1024 * 1024
        ),
    )(tokens, base, down, up, magnitude.reshape(1, UNITS), cotangent)
    return lay, inp, mg.reshape(UNITS), ug, dg


def solution(mesh):
    placed = (
        P(("fsdp", "rep"), None),
        P("fsdp", None),
        P("fsdp", None),
        P(),
        P(),
        P(("fsdp", "rep"), None),
    )
    return jax.shard_map(
        body,
        mesh=mesh,
        in_specs=placed,
        out_specs=(P(("fsdp", "rep"), None), P(("fsdp", "rep"), None), P(), P(), P("fsdp", None)),
        check_vma=False,
    )
```

```python
import math

import jax
import jax.numpy as jnp
from jax import lax
from jax.experimental import pallas as pl
from jax.experimental.pallas import tpu as pltpu
from jax.sharding import PartitionSpec as P

MESH = pl.DeviceIdType.MESH
F32, BF16 = jnp.float32, jnp.bfloat16
TOK, FEAT, UNITS, RANK = 192, 4096, 512, 64
NT = (((1,), (1,)), ((), ()))
TN = (((0,), (0,)), ((), ()))


class Slots:
    def __init__(self):
        self.used = 0

    def take(self, count):
        base = self.used
        self.used += count
        return base


SLOTS = Slots()
LOCAL = SLOTS.take(6)
N_CORE = SLOTS.take(1)
N_Z = SLOTS.take(16)
A_Z = SLOTS.take(16)
A_X = SLOTS.take(4)
A_CORE = SLOTS.take(1)
W_Z = SLOTS.take(16)
W_X = SLOTS.take(4)
W_Y = SLOTS.take(4)
V_X = SLOTS.take(4)
V_Y = SLOTS.take(4)
W_CORE = SLOTS.take(8)
D_CORE = SLOTS.take(1)
D_P = SLOTS.take(16)
D_Q = SLOTS.take(4)
D_O = SLOTS.take(8)
D_G = SLOTS.take(16)
U_CORE = SLOTS.take(1)
U_P = SLOTS.take(16)
U_Q = SLOTS.take(4)
U_O = SLOTS.take(8)
U_G = SLOTS.take(16)
U_GC = SLOTS.take(1)
M_CORE = SLOTS.take(1)
M_P = SLOTS.take(16)
M_Q = SLOTS.take(4)
M_O = SLOTS.take(8)
OUT = SLOTS.take(17)
TOTAL = SLOTS.used


def device(x, y, z, c):
    x, y, z = lax.rem(x + 4, 4), lax.rem(y + 4, 4), lax.rem(z + 32, 32)
    return {"fsdp": lax.rem(z, 16) * 2 + c, "rep": (x * 4 + y) * 2 + z // 16}


def total8(ref):
    return ((ref[0] + ref[1]) + (ref[2] + ref[3])) + ((ref[4] + ref[5]) + (ref[6] + ref[7]))


def kernel(
    tok_hbm, base_hbm, down_hbm, up_hbm, mag_hbm, cot_hbm,
    lay_hbm, inp_hbm, mg_ref, ug_ref, dg_ref,
    tok, own_w, own_a, b_ref, mag, cot,
    wn, wf, ap,
    n_core, n_z,
    scaled_ref, back_ref, lin, lay, inp,
    d_all, d_core, d_half, d_p, d_s, d_q, d_h, d_o, d_g,
    u_all, u_core, u_e, u_p, u_q, u_o, u_g,
    m_core, m_p, m_q, m_o,
    ss, rs,
):
    f_at, r_at = lax.axis_index("fsdp"), lax.axis_index("rep")
    c, zl = lax.rem(f_at, 2), f_at // 2
    zh, xy = lax.rem(r_at, 2), r_at // 2
    x, y, z = xy // 4, lax.rem(xy, 4), zh * 16 + zl
    qb, qa = lax.rem(z, 4), z // 4
    sib = device(x, y, z, 1 - c)
    factor = 1.0 / math.sqrt(196608.0)

    def remote(src, dst, s, r, to):
        return pltpu.make_async_remote_copy(
            src_ref=src, dst_ref=dst, send_sem=ss.at[s], recv_sem=rs.at[r],
            device_id=to, device_id_type=MESH,
        )

    def arrived(dst, r):
        remote(dst, dst, r, r, sib).wait_recv()

    def left_here(src, s):
        remote(src, src, s, s, sib).wait_send()

    def plane(i):
        return lax.rem(x + i // 4, 4), lax.rem(y + lax.rem(i, 4), 4)

    def loop(first, last, step):
        def one(i, _):
            step(i)
            return 0

        lax.fori_loop(first, last, one, 0)

    barrier = pltpu.get_barrier_semaphore()
    near = (-1, 1, -2, 2, -3, 3, -4, 4, -5, 5, -6, 6, -7, 7, -8, 8)
    peers = [device(x, y, z + d, c) for d in near]
    peers += [device(x + i, y + j, z, c) for i in range(4) for j in range(4) if i or j]
    peers += [sib]
    for peer in peers:
        pl.semaphore_signal(barrier, 1, device_id=peer, device_id_type=MESH)

    loads = [
        pltpu.make_async_copy(base_hbm, own_w, rs.at[LOCAL]),
        pltpu.make_async_copy(down_hbm, own_a, rs.at[LOCAL + 1]),
        pltpu.make_async_copy(up_hbm, b_ref, rs.at[LOCAL + 2]),
        pltpu.make_async_copy(mag_hbm, mag, rs.at[LOCAL + 3]),
        pltpu.make_async_copy(cot_hbm, cot, rs.at[LOCAL + 4]),
        pltpu.make_async_copy(tok_hbm, tok, rs.at[LOCAL + 5]),
    ]
    for load in loads:
        load.start()

    loads[0].wait()
    loads[1].wait()
    loads[2].wait()
    merged = own_w[...].astype(F32) + 2.0 * lax.dot_general(
        own_a[...], b_ref[...], TN, preferred_element_type=F32
    )
    n_core[c] = jnp.sum(merged * merged, axis=0, keepdims=True)
    rows_y = pl.ds(pl.multiple_of(y * 32, 32), 32)
    lanes_x = pl.ds(pl.multiple_of(x * 128, 128), 128)
    wn[c, y, x, 4] = own_w[rows_y, lanes_x]
    ap[c, x, zl] = own_a[pl.ds(pl.multiple_of(x * 16, 16), 16), :]
    pl.semaphore_wait(barrier, len(peers))

    n_copy = remote(n_core.at[c], n_core.at[c], N_CORE, N_CORE, sib)
    n_copy.start()
    w_piece = wn.at[c, y, x, 4]

    def w_near(d):
        remote(w_piece, wn.at[c, y, x, 4 - d], W_Z + (4 - d), W_Z + (4 - d), device(x, y, z + d, c)).start()

    def w_far(j):
        d = jnp.where(j < 12, 4 - j, 20 - j)
        remote(w_piece, wf.at[c, x, y, j - 8], W_Z + j, W_Z + j, device(x, y, z + d, c)).start()

    for d in (1, -1, 2, -2, 3, -3, 4):
        w_near(d)
    n_copy.wait()
    n_z[zl] = n_core[0] + n_core[1]

    def z_offset(i):
        return jnp.where(lax.rem(i, 2) == 0, i // 2 + 1, -(i // 2) - 1)

    def n_send(i):
        remote(n_z.at[zl], n_z.at[zl], N_Z + i, N_Z + zl, device(x, y, z + z_offset(i), c)).start()

    loop(0, 15, n_send)
    loop(8, 16, w_far)

    def a_send(i):
        part = ap.at[c, x, zl]
        remote(part, part, A_Z + i, A_Z + zl, device(x, y, z + z_offset(i), c)).start()

    loop(0, 15, a_send)

    for j in (0, 1, 2, 3, 5, 6, 7):
        arrived(wn.at[c, y, x, j], W_Z + j)
    for d in (1, 2, 3):
        part = wn.at[c, y, x]
        remote(part, part, W_X + d, W_X + d, device(x + d, y, z, c)).start()

    def n_wait(i):
        slot = lax.rem(zl - z_offset(i) + 16, 16)
        arrived(n_z.at[slot], N_Z + slot)

    loop(0, 15, n_wait)
    loads[3].wait()
    loads[4].wait()
    squares = jnp.sum(n_z[...], axis=0)
    col_norm = jnp.sqrt(squares + 1e-06)
    scaling = mag[...] / col_norm
    scaled = (cot[...].astype(F32) * scaling).astype(BF16)
    scaled_ref[...] = scaled
    back = lax.dot_general(scaled, b_ref[...], NT, preferred_element_type=F32).astype(BF16)
    back_ref[...] = back
    back_t = (back.astype(F32).T).astype(BF16)
    loads[5].wait()

    def d_part(k_at):
        for n in range(4):
            part = (2.0 * factor) * jnp.dot(
                back_t, tok[:, n * 1024 : n * 1024 + 1024], preferred_element_type=F32
            )
            for r in range(4):
                for k in range(2):
                    at = r * 256 + k * 128
                    d_all[k, :, n, r] = part[:, at : at + 128].reshape(4, 16, 128)

    d_part(0)
    d_core_copy = remote(d_all.at[1 - c], d_core, D_CORE, D_CORE, sib)
    d_core_copy.start()

    for j in range(8, 16):
        arrived(wf.at[c, x, y, j - 8], W_Z + j)
    for d in (1, 2, 3):
        part = wf.at[c, x, y]
        remote(part, part, V_Y + d, V_Y + d, device(x, y + d, z, c)).start()

    def around(at, d):
        return lax.rem(at + d + 4, 4)

    def block_send(buf, at, base_sem, core_sem, ahead, behind):
        block = buf.at[c, at]
        remote(block, block, base_sem, base_sem, ahead).start()
        remote(block, block, base_sem + 1, base_sem + 1, behind).start()
        remote(block, block, core_sem, core_sem, sib).start()

    def block_forward(buf, at, base_sem, core_sem, ahead, behind):
        before, after = around(at, -1), around(at, 1)
        arrived(buf.at[c, before], base_sem)
        half = buf.at[c, before, 0:2]
        remote(half, half, base_sem + 2, base_sem + 2, ahead).start()
        arrived(buf.at[c, after], base_sem + 1)
        half = buf.at[c, after, 2:4]
        remote(half, half, base_sem + 3, base_sem + 3, behind).start()
        remote(buf.at[c, before], buf.at[c, before], core_sem + 1, core_sem + 1, sib).start()
        remote(buf.at[c, after], buf.at[c, after], core_sem + 2, core_sem + 2, sib).start()

    def block_last(buf, at, base_sem, core_sem):
        last = around(at, 2)
        arrived(buf.at[c, last, 0:2], base_sem + 2)
        arrived(buf.at[c, last, 2:4], base_sem + 3)
        remote(buf.at[c, last], buf.at[c, last], core_sem + 3, core_sem + 3, sib).start()

    def block_core(buf, at, core_sem):
        for n, d in enumerate((0, -1, 1, 2)):
            arrived(buf.at[1 - c, around(at, d)], core_sem + n)

    def block_sent(buf, at, base_sem, core_sem):
        left_here(buf.at[c, at], base_sem)
        left_here(buf.at[c, at], base_sem + 1)
        left_here(buf.at[c, at, 0:2], base_sem + 2)
        left_here(buf.at[c, at, 2:4], base_sem + 3)
        for n in range(4):
            left_here(buf.at[c, at], core_sem + n)

    near_y = (wn, y, W_Y, W_CORE)
    far_x = (wf, x, V_X, W_CORE + 4)
    y_ahead, y_behind = device(x, y + 1, z, c), device(x, y - 1, z, c)
    x_ahead, x_behind = device(x + 1, y, z, c), device(x - 1, y, z, c)

    for d in (1, 2, 3):
        arrived(wn.at[c, y, lax.rem(x - d + 4, 4)], W_X + d)
    block_send(*near_y, y_ahead, y_behind)

    d_core_copy.wait()
    for i in range(4):
        d_half[i] = (d_core[i] + d_all[c, i]).astype(BF16)

    def d_send(i):
        px, py = plane(i)
        remote(d_half.at[px, py], d_p.at[xy], D_P + i, D_P + xy, device(px, py, z, c)).start()

    loop(1, 16, d_send)
    d_p[xy] = d_half[x, y]

    def a_wait(i):
        slot = lax.rem(zl - z_offset(i) + 16, 16)
        arrived(ap.at[c, x, slot], A_Z + slot)

    loop(0, 15, a_wait)
    for d in (1, 2, 3):
        remote(ap.at[c, x], ap.at[c, x], A_X + d, A_X + d, device(x + d, y, z, c)).start()

    for d in (1, 2, 3):
        arrived(wf.at[c, x, lax.rem(y - d + 4, 4)], V_Y + d)
    block_send(*far_x, x_ahead, x_behind)
    block_forward(*near_y, y_ahead, y_behind)

    for d in (1, 2, 3):
        arrived(ap.at[c, lax.rem(x - d + 4, 4)], A_X + d)
    a_core_copy = remote(ap.at[c], ap.at[c], A_CORE, A_CORE, sib)
    a_core_copy.start()

    def d_wait(i):
        px, py = plane(i)
        arrived(d_p.at[px * 4 + py], D_P + px * 4 + py)

    loop(1, 16, d_wait)
    for r in range(4):
        d_s[r] = jnp.sum(d_p[:, r].astype(F32), axis=0)
    for d in (1, 2, 3):
        to = lax.rem(qb + d, 4)
        remote(d_s.at[to], d_q.at[qb], D_Q + d, D_Q + d, device(x, y, qa * 4 + to, c)).start()
    d_q[qb] = d_s[qb]

    block_forward(*far_x, x_ahead, x_behind)

    def columns(res):
        return pl.ds(pl.multiple_of(res * 256, 256), 256)

    def a_pair(res):
        return jnp.concatenate([ap[0, :, res].reshape(64, 128), ap[1, :, res].reshape(64, 128)], axis=1)

    arrived(ap.at[1 - c], A_CORE)
    low_sum = jnp.zeros((TOK, RANK), F32)
    for n in range(4):
        a_four = jnp.concatenate([a_pair(n * 4 + r) for r in range(4)], axis=1)
        low_sum = low_sum + lax.dot_general(
            tok[:, n * 1024 : n * 1024 + 1024], a_four, NT, preferred_element_type=F32
        )
    low = low_sum.astype(BF16)
    up_part = (2.0 * factor) * lax.dot_general(low, scaled_ref[...], TN, preferred_element_type=F32)
    for k in range(2):
        for q in range(4):
            u_all[k, q] = up_part[k * 32 : k * 32 + 32, q * 128 : q * 128 + 128].reshape(4, 8, 128)
    u_core_copy = remote(u_all.at[1 - c], u_core, U_CORE, U_CORE, sib)
    u_core_copy.start()
    lin[...] = 2.0 * jnp.dot(low, b_ref[...], preferred_element_type=F32)

    block_last(*near_y)

    owner = lax.rem(qa, 4) == y
    for d in (1, 2, 3):
        arrived(d_q.at[lax.rem(qb - d + 4, 4)], D_Q + d)
    d_h[...] = (d_q[0] + d_q[1]) + (d_q[2] + d_q[3])
    for hi in (0, 1):
        to = y + 4 * hi

        @pl.when(to != qa)
        def _():
            remote(d_h, d_o.at[qa], D_O + hi, D_O + qa, device(x, y, to * 4 + qb, c)).start()

    u_core_copy.wait()
    u_e[...] = u_all[c] + u_core[...]

    def u_send(i):
        px, py = plane(i)
        remote(u_e.at[px, py], u_p.at[xy], U_P + i, U_P + xy, device(px, py, z, c)).start()

    loop(1, 16, u_send)
    u_p[xy] = u_e[x, y]

    block_last(*far_x)

    def near_pair(j):
        return jnp.concatenate([wn[:, :, q, j].reshape(256, 128) for q in range(4)], axis=1)

    def far_pair(j):
        return jnp.concatenate([wf[:, q, :, j].reshape(256, 128) for q in range(4)], axis=1)

    def near_at(j):
        return lax.rem(zl + j + 12, 16)

    def far_at(j):
        return lax.rem(zl + j + 20, 16)

    def forward(pair, at):
        def two(i):
            j = i * 2
            first = jnp.dot(tok[:, columns(at(j))], pair(j), preferred_element_type=F32)
            second = jnp.dot(tok[:, columns(at(j + 1))], pair(j + 1), preferred_element_type=F32)
            lin[...] += first + second

        loop(0, 4, two)

    def backward(pair, at, first, last):
        def one(j):
            res = at(j)
            grad = lax.dot_general(scaled_ref[...], pair(j), NT, preferred_element_type=F32)
            grad = grad + 2.0 * jnp.dot(back_ref[...], a_pair(res), preferred_element_type=F32)
            inp[:, columns(res)] = grad.astype(BF16)
            pltpu.make_async_copy(
                inp.at[:, columns(res)], inp_hbm.at[:, columns(res)], rs.at[OUT + res]
            ).start()

        loop(first, last, one)

    block_core(wn, y, W_CORE)
    forward(near_pair, near_at)

    def u_wait(i):
        px, py = plane(i)
        arrived(u_p.at[px * 4 + py], U_P + px * 4 + py)

    loop(1, 16, u_wait)
    u_q[qb] = jnp.sum(u_p[...], axis=0)
    for d in (1, 2, 3):
        to = lax.rem(qb + d, 4)
        remote(u_q.at[qb], u_q.at[qb], U_Q + d, U_Q + d, device(x, y, qa * 4 + to, c)).start()

    block_core(wf, x, W_CORE + 4)
    forward(far_pair, far_at)

    m_core[c] = jnp.sum(cot[...].astype(F32) * lin[...], axis=0, keepdims=True)
    m_core_copy = remote(m_core.at[c], m_core.at[c], M_CORE, M_CORE, sib)
    m_core_copy.start()
    backward(near_pair, near_at, 0, 4)
    m_core_copy.wait()
    m_p[xy] = m_core[0] + m_core[1]

    def m_send(i):
        px, py = plane(i)
        remote(m_p.at[xy], m_p.at[xy], M_P + i, M_P + xy, device(px, py, z, c)).start()

    loop(1, 16, m_send)

    for d in (1, 2, 3):
        arrived(u_q.at[lax.rem(qb - d + 4, 4)], U_Q + d)
    u_o[qa] = (u_q[0] + u_q[1]) + (u_q[2] + u_q[3])
    for d in range(1, 8):
        to = lax.rem(qa + d, 8)
        remote(u_o.at[qa], u_o.at[qa], U_O + d, U_O + d, device(x, y, to * 4 + qb, c)).start()

    backward(near_pair, near_at, 4, 8)

    @pl.when(owner)
    def _():
        d_o[qa] = d_h[...]
        for d in range(1, 8):
            at = lax.rem(qa - d + 8, 8)
            arrived(d_o.at[at], D_O + at)
        d_g[x] = total8(d_o)

        def g_send(i):
            px, py = plane(i)
            remote(d_g.at[x], d_g.at[x], D_G + i, D_G + x, device(px, py, z, c)).start()

        loop(1, 16, g_send)

    def m_wait(i):
        px, py = plane(i)
        arrived(m_p.at[px * 4 + py], M_P + px * 4 + py)

    loop(1, 16, m_wait)
    m_q[qb] = jnp.sum(m_p[...], axis=0)
    for d in (1, 2, 3):
        to = lax.rem(qb + d, 4)
        remote(m_q.at[qb], m_q.at[qb], M_Q + d, M_Q + d, device(x, y, qa * 4 + to, c)).start()
    lay[...] = (lin[...] * scaling).astype(BF16)
    lay_copy = pltpu.make_async_copy(lay, lay_hbm, rs.at[OUT + 16])
    lay_copy.start()
    backward(far_pair, far_at, 0, 3)
    for d in (1, 2, 3):
        arrived(m_q.at[lax.rem(qb - d + 4, 4)], M_Q + d)
    m_o[qa] = (m_q[0] + m_q[1]) + (m_q[2] + m_q[3])
    for d in range(1, 8):
        to = lax.rem(qa + d, 8)
        remote(m_o.at[qa], m_o.at[qa], M_O + d, M_O + d, device(x, y, to * 4 + qb, c)).start()

    for d in range(1, 8):
        arrived(u_o.at[lax.rem(qa - d + 8, 8)], U_O + d)
    u_g[c, xy] = total8(u_o)

    def ug_send(i):
        px, py = plane(i)
        part = u_g.at[c, xy]
        remote(part, part, U_G + i, U_G + xy, device(px, py, z, c)).start()

    loop(1, 16, ug_send)

    backward(far_pair, far_at, 3, 8)

    def ug_wait(i):
        px, py = plane(i)
        arrived(u_g.at[c, px * 4 + py], U_G + px * 4 + py)

    loop(1, 16, ug_wait)
    ug_copy = remote(u_g.at[c], u_g.at[c], U_GC, U_GC, sib)
    ug_copy.start()

    def dg_wait(i):
        @pl.when(jnp.logical_or(i != x, jnp.logical_not(owner)))
        def _():
            arrived(d_g.at[i], D_G + i)

    loop(0, 4, dg_wait)
    dg_ref[...] = d_g[...].reshape(64, 128)
    ug_copy.wait()
    for k in range(2):
        for q in range(4):
            ug_ref[k * 32 : k * 32 + 32, q * 128 : q * 128 + 128] = u_g[
                k, q * 4 : q * 4 + 4
            ].reshape(32, 128)

    def sent(i):
        left_here(n_z.at[zl], N_Z + i)
        left_here(ap.at[c, x, zl], A_Z + i)
        left_here(d_p.at[0], D_P + i + 1)
        left_here(u_p.at[0], U_P + i + 1)
        left_here(m_p.at[xy], M_P + i + 1)
        left_here(u_g.at[c, xy], U_G + i + 1)

        @pl.when(owner)
        def _():
            left_here(d_g.at[x], D_G + i + 1)

    loop(0, 15, sent)
    for j in (0, 1, 2, 3, *range(5, 16)):
        left_here(w_piece, W_Z + j)
    for d in (1, 2, 3):
        left_here(ap.at[c, x], A_X + d)
        left_here(wn.at[c, y, x], W_X + d)
        left_here(wf.at[c, x, y], V_Y + d)
        left_here(d_s.at[0], D_Q + d)
        left_here(u_q.at[0], U_Q + d)
        left_here(m_q.at[0], M_Q + d)
    for hi in (0, 1):

        @pl.when(y + 4 * hi != qa)
        def _():
            left_here(d_h, D_O + hi)

    for d in range(1, 8):
        left_here(u_o.at[0], U_O + d)
        left_here(m_o.at[0], M_O + d)
    left_here(ap.at[c], A_CORE)
    block_sent(*near_y)
    block_sent(*far_x)
    lay_copy.wait()

    def stored(i):
        pltpu.make_async_copy(
            inp.at[:, columns(i)], inp_hbm.at[:, columns(i)], rs.at[OUT + i]
        ).wait()

    loop(0, 16, stored)

    for d in range(1, 8):
        arrived(m_o.at[lax.rem(qa - d + 8, 8)], M_O + d)
    mg_ref[...] = total8(m_o) / col_norm * factor


def hand_over(*refs):
    sources, targets, held, came, went = refs[:5], refs[5:10], refs[10:15], refs[15], refs[16]
    parts = []
    for i in (1, 0, 3, 4, 2):
        rows = sources[i].shape[0]
        step = 48 if i == 1 else rows
        for first in range(0, rows, step):
            at = pl.ds(first, step)
            parts.append((sources[i].at[at], held[i].at[at], targets[i].at[at]))
    into = [pltpu.make_async_copy(p[0], p[1], came.at[n]) for n, p in enumerate(parts)]
    out = [pltpu.make_async_copy(p[1], p[2], went.at[n]) for n, p in enumerate(parts)]
    for copy in into:
        copy.start()
    for first, second in zip(into, out):
        first.wait()
        second.start()
    for copy in out:
        copy.wait()


def body(tokens, base, down, up, magnitude, cotangent):
    anywhere = pl.BlockSpec(memory_space=pl.ANY)
    vmem = pl.BlockSpec(memory_space=pltpu.VMEM)
    shapes = (
        jax.ShapeDtypeStruct((TOK, UNITS), BF16),
        jax.ShapeDtypeStruct((TOK, FEAT), BF16),
        jax.ShapeDtypeStruct((1, UNITS), F32),
        jax.ShapeDtypeStruct((RANK, UNITS), F32),
        jax.ShapeDtypeStruct((RANK, 128), F32),
    )
    results = pl.pallas_call(
        kernel,
        out_shape=shapes,
        in_specs=[anywhere] * 6,
        out_specs=(anywhere, anywhere, vmem, vmem, vmem),
        scratch_shapes=[
            pltpu.VMEM((TOK, FEAT), BF16),
            pltpu.VMEM((128, UNITS), BF16),
            pltpu.VMEM((RANK, 128), BF16),
            pltpu.VMEM((RANK, UNITS), BF16),
            pltpu.VMEM((1, UNITS), F32),
            pltpu.VMEM((TOK, UNITS), BF16),
            pltpu.VMEM((2, 4, 4, 8, 32, 128), BF16),
            pltpu.VMEM((2, 4, 4, 8, 32, 128), BF16),
            pltpu.VMEM((2, 4, 16, 16, 128), BF16),
            pltpu.VMEM((2, 1, UNITS), F32),
            pltpu.VMEM((16, 1, UNITS), F32),
            pltpu.VMEM((TOK, UNITS), BF16),
            pltpu.VMEM((TOK, RANK), BF16),
            pltpu.VMEM((TOK, UNITS), F32),
            pltpu.VMEM((TOK, UNITS), BF16),
            pltpu.VMEM((TOK, FEAT), BF16),
            pltpu.VMEM((2, 4, 4, 4, 16, 128), F32),
            pltpu.VMEM((4, 4, 4, 16, 128), F32),
            pltpu.VMEM((4, 4, 4, 16, 128), BF16),
            pltpu.VMEM((16, 4, 16, 128), BF16),
            pltpu.VMEM((4, 16, 128), F32),
            pltpu.VMEM((4, 16, 128), F32),
            pltpu.VMEM((16, 128), F32),
            pltpu.VMEM((8, 16, 128), F32),
            pltpu.VMEM((4, 16, 128), F32),
            pltpu.VMEM((2, 4, 4, 8, 128), F32),
            pltpu.VMEM((4, 4, 8, 128), F32),
            pltpu.VMEM((4, 4, 8, 128), F32),
            pltpu.VMEM((16, 8, 128), F32),
            pltpu.VMEM((4, 8, 128), F32),
            pltpu.VMEM((8, 8, 128), F32),
            pltpu.VMEM((2, 16, 8, 128), F32),
            pltpu.VMEM((2, 1, UNITS), F32),
            pltpu.VMEM((16, 1, UNITS), F32),
            pltpu.VMEM((4, 1, UNITS), F32),
            pltpu.VMEM((8, 1, UNITS), F32),
            pltpu.SemaphoreType.DMA((TOTAL,)),
            pltpu.SemaphoreType.DMA((TOTAL,)),
        ],
        compiler_params=pltpu.CompilerParams(
            collective_id=0, has_side_effects=True, vmem_limit_bytes=60 * 1024 * 1024
        ),
    )(tokens, base, down.T, up, magnitude.reshape(1, UNITS), cotangent)
    lay, inp, mg, ug, dg = pl.pallas_call(
        hand_over,
        out_shape=shapes,
        in_specs=[anywhere] * 5,
        out_specs=(anywhere,) * 5,
        scratch_shapes=[pltpu.VMEM(shape.shape, shape.dtype) for shape in shapes]
        + [pltpu.SemaphoreType.DMA((8,)), pltpu.SemaphoreType.DMA((8,))],
        compiler_params=pltpu.CompilerParams(vmem_limit_bytes=60 * 1024 * 1024),
    )(*results)
    return lay, inp, mg.reshape(UNITS), ug, dg.T


def solution(mesh):
    placed = (
        P(("fsdp", "rep"), None),
        P("fsdp", None),
        P("fsdp", None),
        P(),
        P(),
        P(("fsdp", "rep"), None),
    )
    return jax.shard_map(
        body,
        mesh=mesh,
        in_specs=placed,
        out_specs=(P(("fsdp", "rep"), None), P(("fsdp", "rep"), None), P(), P(), P("fsdp", None)),
        check_vma=False,
    )
```

```python
import math

import jax
import jax.numpy as jnp
from jax import lax
from jax.experimental import pallas as pl
from jax.experimental.pallas import tpu as pltpu
from jax.sharding import PartitionSpec as P

MESH = pl.DeviceIdType.MESH
F32, BF16 = jnp.float32, jnp.bfloat16
TOK, FEAT, UNITS, RANK = 192, 4096, 512, 64
NT = (((1,), (1,)), ((), ()))
TN = (((0,), (0,)), ((), ()))


class Slots:
    def __init__(self):
        self.used = 0

    def take(self, count):
        base = self.used
        self.used += count
        return base


SLOTS = Slots()
LOCAL = SLOTS.take(6)
N_CORE = SLOTS.take(1)
N_Z = SLOTS.take(16)
A_Z = SLOTS.take(16)
A_X = SLOTS.take(4)
A_CORE = SLOTS.take(1)
W_Z = SLOTS.take(16)
W_X = SLOTS.take(4)
W_Y = SLOTS.take(4)
V_X = SLOTS.take(4)
V_Y = SLOTS.take(4)
W_CORE = SLOTS.take(8)
W_PA = SLOTS.take(4)
W_PB = SLOTS.take(4)
V_PA = SLOTS.take(4)
V_PB = SLOTS.take(4)
D_CORE = SLOTS.take(1)
D_P = SLOTS.take(16)
D_Q = SLOTS.take(4)
D_O = SLOTS.take(8)
D_G = SLOTS.take(16)
U_CORE = SLOTS.take(1)
U_P = SLOTS.take(16)
U_Q = SLOTS.take(4)
U_O = SLOTS.take(8)
U_G = SLOTS.take(16)
U_GC = SLOTS.take(1)
M_CORE = SLOTS.take(1)
M_P = SLOTS.take(16)
M_Q = SLOTS.take(4)
M_O = SLOTS.take(8)
OUT = SLOTS.take(17)
TOTAL = SLOTS.used


def device(x, y, z, c):
    x, y, z = lax.rem(x + 4, 4), lax.rem(y + 4, 4), lax.rem(z + 32, 32)
    return {"fsdp": lax.rem(z, 16) * 2 + c, "rep": (x * 4 + y) * 2 + z // 16}


def total8(ref):
    return ((ref[0] + ref[1]) + (ref[2] + ref[3])) + ((ref[4] + ref[5]) + (ref[6] + ref[7]))


def kernel(
    tok_hbm, base_hbm, down_hbm, up_hbm, mag_hbm, cot_hbm,
    lay_hbm, inp_hbm, mg_ref, ug_ref, dg_ref,
    tok, own_w, own_a, b_ref, mag, cot,
    wn, wf, ap,
    n_core, n_z,
    scaled_ref, back_ref, lin, lay, inp,
    d_all, d_core, d_half, d_p, d_s, d_q, d_h, d_o, d_g,
    u_all, u_core, u_e, u_p, u_q, u_o, u_g,
    m_core, m_p, m_q, m_o,
    ss, rs,
):
    f_at, r_at = lax.axis_index("fsdp"), lax.axis_index("rep")
    c, zl = lax.rem(f_at, 2), f_at // 2
    zh, xy = lax.rem(r_at, 2), r_at // 2
    x, y, z = xy // 4, lax.rem(xy, 4), zh * 16 + zl
    qb, qa = lax.rem(z, 4), z // 4
    sib = device(x, y, z, 1 - c)
    factor = 1.0 / math.sqrt(196608.0)

    def remote(src, dst, s, r, to):
        return pltpu.make_async_remote_copy(
            src_ref=src, dst_ref=dst, send_sem=ss.at[s], recv_sem=rs.at[r],
            device_id=to, device_id_type=MESH,
        )

    def arrived(dst, r):
        remote(dst, dst, r, r, sib).wait_recv()

    def left_here(src, s):
        remote(src, src, s, s, sib).wait_send()

    def plane(i):
        return lax.rem(x + i // 4, 4), lax.rem(y + lax.rem(i, 4), 4)

    def loop(first, last, step):
        def one(i, _):
            step(i)
            return 0

        lax.fori_loop(first, last, one, 0)

    barrier = pltpu.get_barrier_semaphore()
    near = (-1, 1, -2, 2, -3, 3, -4, 4, -5, 5, -6, 6, -7, 7, -8, 8)
    peers = [device(x, y, z + d, c) for d in near]
    peers += [device(x + i, y + j, z, c) for i in range(4) for j in range(4) if i or j]
    peers += [sib]
    for peer in peers:
        pl.semaphore_signal(barrier, 1, device_id=peer, device_id_type=MESH)

    loads = [
        pltpu.make_async_copy(base_hbm, own_w, rs.at[LOCAL]),
        pltpu.make_async_copy(down_hbm, own_a, rs.at[LOCAL + 1]),
        pltpu.make_async_copy(up_hbm, b_ref, rs.at[LOCAL + 2]),
        pltpu.make_async_copy(mag_hbm, mag, rs.at[LOCAL + 3]),
        pltpu.make_async_copy(cot_hbm, cot, rs.at[LOCAL + 4]),
        pltpu.make_async_copy(tok_hbm, tok, rs.at[LOCAL + 5]),
    ]
    for load in loads:
        load.start()

    loads[0].wait()
    loads[1].wait()
    loads[2].wait()
    merged = own_w[...].astype(F32) + 2.0 * lax.dot_general(
        own_a[...], b_ref[...], TN, preferred_element_type=F32
    )
    n_core[c] = jnp.sum(merged * merged, axis=0, keepdims=True)
    rows_y = pl.ds(pl.multiple_of(y * 32, 32), 32)
    lanes_x = pl.ds(pl.multiple_of(x * 128, 128), 128)
    wn[c, y, x, 4] = own_w[rows_y, lanes_x]
    ap[c, x, zl] = own_a[pl.ds(pl.multiple_of(x * 16, 16), 16), :]
    pl.semaphore_wait(barrier, len(peers))

    n_copy = remote(n_core.at[c], n_core.at[c], N_CORE, N_CORE, sib)
    n_copy.start()
    w_piece = wn.at[c, y, x, 4]

    def w_near(d):
        remote(w_piece, wn.at[c, y, x, 4 - d], W_Z + (4 - d), W_Z + (4 - d), device(x, y, z + d, c)).start()

    def w_far(j):
        d = jnp.where(j < 12, 4 - j, 20 - j)
        remote(w_piece, wf.at[c, x, y, j - 8], W_Z + j, W_Z + j, device(x, y, z + d, c)).start()

    y_ahead, y_behind = device(x, y + 1, z, c), device(x, y - 1, z, c)
    x_ahead, x_behind = device(x + 1, y, z, c), device(x - 1, y, z, c)

    def near_piece(p):
        part = wn.at[c, y, p]
        remote(part, part, W_PA + p, W_PA + p, y_ahead).start()
        remote(part, part, W_PB + p, W_PB + p, y_behind).start()

    def far_piece(p):
        part = wf.at[c, x, p]
        remote(part, part, V_PA + p, V_PA + p, x_ahead).start()
        remote(part, part, V_PB + p, V_PB + p, x_behind).start()

    for d in (1, -1, 2, -2, 3, -3, 4):
        w_near(d)
    n_copy.wait()
    n_z[zl] = n_core[0] + n_core[1]

    def z_offset(i):
        return jnp.where(lax.rem(i, 2) == 0, i // 2 + 1, -(i // 2) - 1)

    def n_send(i):
        remote(n_z.at[zl], n_z.at[zl], N_Z + i, N_Z + zl, device(x, y, z + z_offset(i), c)).start()

    loop(0, 15, n_send)
    loop(8, 16, w_far)

    def a_send(i):
        part = ap.at[c, x, zl]
        remote(part, part, A_Z + i, A_Z + zl, device(x, y, z + z_offset(i), c)).start()

    loop(0, 15, a_send)

    for j in (0, 1, 2, 3, 5, 6, 7):
        arrived(wn.at[c, y, x, j], W_Z + j)
    for d in (1, 2, 3):
        part = wn.at[c, y, x]
        remote(part, part, W_X + d, W_X + d, device(x + d, y, z, c)).start()
    near_piece(x)

    def n_wait(i):
        slot = lax.rem(zl - z_offset(i) + 16, 16)
        arrived(n_z.at[slot], N_Z + slot)

    loop(0, 15, n_wait)
    loads[3].wait()
    loads[4].wait()
    squares = jnp.sum(n_z[...], axis=0)
    col_norm = jnp.sqrt(squares + 1e-06)
    scaling = mag[...] / col_norm
    scaled = (cot[...].astype(F32) * scaling).astype(BF16)
    scaled_ref[...] = scaled
    back = lax.dot_general(scaled, b_ref[...], NT, preferred_element_type=F32).astype(BF16)
    back_ref[...] = back
    back_t = (back.astype(F32).T).astype(BF16)
    loads[5].wait()

    def d_part(k_at):
        for n in range(4):
            part = (2.0 * factor) * jnp.dot(
                back_t, tok[:, n * 1024 : n * 1024 + 1024], preferred_element_type=F32
            )
            for r in range(4):
                for k in range(2):
                    at = r * 256 + k * 128
                    d_all[k, :, n, r] = part[:, at : at + 128].reshape(4, 16, 128)

    d_part(0)
    d_core_copy = remote(d_all.at[1 - c], d_core, D_CORE, D_CORE, sib)
    d_core_copy.start()

    for j in range(8, 16):
        arrived(wf.at[c, x, y, j - 8], W_Z + j)
    for d in (1, 2, 3):
        part = wf.at[c, x, y]
        remote(part, part, V_Y + d, V_Y + d, device(x, y + d, z, c)).start()
    far_piece(y)

    def around(at, d):
        return lax.rem(at + d + 4, 4)

    def block_send(buf, at, core_sem):
        block = buf.at[c, at]
        remote(block, block, core_sem, core_sem, sib).start()

    def block_forward(buf, at, base_sem, core_sem, pa, pb, ahead, behind):
        before, after = around(at, -1), around(at, 1)
        for p in range(2):
            arrived(buf.at[c, before, p], pa + p)
        half = buf.at[c, before, 0:2]
        remote(half, half, base_sem + 2, base_sem + 2, ahead).start()
        for p in range(2, 4):
            arrived(buf.at[c, after, p], pb + p)
        half = buf.at[c, after, 2:4]
        remote(half, half, base_sem + 3, base_sem + 3, behind).start()
        for p in range(2):
            arrived(buf.at[c, before, 2 + p], pa + (2 + p))
            arrived(buf.at[c, after, p], pb + p)
        remote(buf.at[c, before], buf.at[c, before], core_sem + 1, core_sem + 1, sib).start()
        remote(buf.at[c, after], buf.at[c, after], core_sem + 2, core_sem + 2, sib).start()

    def block_last(buf, at, base_sem, core_sem):
        last = around(at, 2)
        arrived(buf.at[c, last, 0:2], base_sem + 2)
        arrived(buf.at[c, last, 2:4], base_sem + 3)
        remote(buf.at[c, last], buf.at[c, last], core_sem + 3, core_sem + 3, sib).start()

    def block_core(buf, at, core_sem):
        for n, d in enumerate((0, -1, 1, 2)):
            arrived(buf.at[1 - c, around(at, d)], core_sem + n)

    def block_sent(buf, at, base_sem, core_sem, pa, pb):
        for p in range(4):
            left_here(buf.at[c, at, p], pa + p)
            left_here(buf.at[c, at, p], pb + p)
        left_here(buf.at[c, at, 0:2], base_sem + 2)
        left_here(buf.at[c, at, 2:4], base_sem + 3)
        for n in range(4):
            left_here(buf.at[c, at], core_sem + n)

    near_y = (wn, y, W_Y, W_CORE)
    far_x = (wf, x, V_X, W_CORE + 4)
    for d in (1, 3, 2):
        arrived(wn.at[c, y, around(x, -d)], W_X + d)
        near_piece(around(x, -d))
    block_send(wn, y, W_CORE)

    d_core_copy.wait()
    for i in range(4):
        d_half[i] = (d_core[i] + d_all[c, i]).astype(BF16)

    def d_send(i):
        px, py = plane(i)
        remote(d_half.at[px, py], d_p.at[xy], D_P + i, D_P + xy, device(px, py, z, c)).start()

    loop(1, 16, d_send)
    d_p[xy] = d_half[x, y]

    def a_wait(i):
        slot = lax.rem(zl - z_offset(i) + 16, 16)
        arrived(ap.at[c, x, slot], A_Z + slot)

    loop(0, 15, a_wait)
    for d in (1, 2, 3):
        remote(ap.at[c, x], ap.at[c, x], A_X + d, A_X + d, device(x + d, y, z, c)).start()

    for d in (1, 3, 2):
        arrived(wf.at[c, x, around(y, -d)], V_Y + d)
        far_piece(around(y, -d))
    block_send(wf, x, W_CORE + 4)
    block_forward(*near_y, W_PA, W_PB, y_ahead, y_behind)

    for d in (1, 2, 3):
        arrived(ap.at[c, lax.rem(x - d + 4, 4)], A_X + d)
    a_core_copy = remote(ap.at[c], ap.at[c], A_CORE, A_CORE, sib)
    a_core_copy.start()

    def d_wait(i):
        px, py = plane(i)
        arrived(d_p.at[px * 4 + py], D_P + px * 4 + py)

    loop(1, 16, d_wait)
    for r in range(4):
        d_s[r] = jnp.sum(d_p[:, r].astype(F32), axis=0)
    for d in (1, 2, 3):
        to = lax.rem(qb + d, 4)
        remote(d_s.at[to], d_q.at[qb], D_Q + d, D_Q + d, device(x, y, qa * 4 + to, c)).start()
    d_q[qb] = d_s[qb]

    block_forward(*far_x, V_PA, V_PB, x_ahead, x_behind)

    def columns(res):
        return pl.ds(pl.multiple_of(res * 256, 256), 256)

    def a_pair(res):
        return jnp.concatenate([ap[0, :, res].reshape(64, 128), ap[1, :, res].reshape(64, 128)], axis=1)

    arrived(ap.at[1 - c], A_CORE)
    low_sum = jnp.zeros((TOK, RANK), F32)
    for n in range(4):
        a_four = jnp.concatenate([a_pair(n * 4 + r) for r in range(4)], axis=1)
        low_sum = low_sum + lax.dot_general(
            tok[:, n * 1024 : n * 1024 + 1024], a_four, NT, preferred_element_type=F32
        )
    low = low_sum.astype(BF16)
    up_part = (2.0 * factor) * lax.dot_general(low, scaled_ref[...], TN, preferred_element_type=F32)
    for k in range(2):
        for q in range(4):
            u_all[k, q] = up_part[k * 32 : k * 32 + 32, q * 128 : q * 128 + 128].reshape(4, 8, 128)
    u_core_copy = remote(u_all.at[1 - c], u_core, U_CORE, U_CORE, sib)
    u_core_copy.start()
    lin[...] = 2.0 * jnp.dot(low, b_ref[...], preferred_element_type=F32)

    block_last(*near_y)

    owner = lax.rem(qa, 4) == y
    for d in (1, 2, 3):
        arrived(d_q.at[lax.rem(qb - d + 4, 4)], D_Q + d)
    d_h[...] = (d_q[0] + d_q[1]) + (d_q[2] + d_q[3])
    for hi in (0, 1):
        to = y + 4 * hi

        @pl.when(to != qa)
        def _():
            remote(d_h, d_o.at[qa], D_O + hi, D_O + qa, device(x, y, to * 4 + qb, c)).start()

    u_core_copy.wait()
    u_e[...] = u_all[c] + u_core[...]

    def u_send(i):
        px, py = plane(i)
        remote(u_e.at[px, py], u_p.at[xy], U_P + i, U_P + xy, device(px, py, z, c)).start()

    loop(1, 16, u_send)
    u_p[xy] = u_e[x, y]

    block_last(*far_x)

    def near_pair(j):
        return jnp.concatenate([wn[:, :, q, j].reshape(256, 128) for q in range(4)], axis=1)

    def far_pair(j):
        return jnp.concatenate([wf[:, q, :, j].reshape(256, 128) for q in range(4)], axis=1)

    def near_at(j):
        return lax.rem(zl + j + 12, 16)

    def far_at(j):
        return lax.rem(zl + j + 20, 16)

    def forward(pair, at):
        def two(i):
            j = i * 2
            first = jnp.dot(tok[:, columns(at(j))], pair(j), preferred_element_type=F32)
            second = jnp.dot(tok[:, columns(at(j + 1))], pair(j + 1), preferred_element_type=F32)
            lin[...] += first + second

        loop(0, 4, two)

    def backward(pair, at, first, last):
        def one(j):
            res = at(j)
            grad = lax.dot_general(scaled_ref[...], pair(j), NT, preferred_element_type=F32)
            grad = grad + 2.0 * jnp.dot(back_ref[...], a_pair(res), preferred_element_type=F32)
            inp[:, columns(res)] = grad.astype(BF16)
            pltpu.make_async_copy(
                inp.at[:, columns(res)], inp_hbm.at[:, columns(res)], rs.at[OUT + res]
            ).start()

        loop(first, last, one)

    block_core(wn, y, W_CORE)
    forward(near_pair, near_at)

    def u_wait(i):
        px, py = plane(i)
        arrived(u_p.at[px * 4 + py], U_P + px * 4 + py)

    loop(1, 16, u_wait)
    u_q[qb] = jnp.sum(u_p[...], axis=0)
    for d in (1, 2, 3):
        to = lax.rem(qb + d, 4)
        remote(u_q.at[qb], u_q.at[qb], U_Q + d, U_Q + d, device(x, y, qa * 4 + to, c)).start()

    block_core(wf, x, W_CORE + 4)
    forward(far_pair, far_at)

    m_core[c] = jnp.sum(cot[...].astype(F32) * lin[...], axis=0, keepdims=True)
    m_core_copy = remote(m_core.at[c], m_core.at[c], M_CORE, M_CORE, sib)
    m_core_copy.start()
    backward(near_pair, near_at, 0, 4)
    m_core_copy.wait()
    m_p[xy] = m_core[0] + m_core[1]

    def m_send(i):
        px, py = plane(i)
        remote(m_p.at[xy], m_p.at[xy], M_P + i, M_P + xy, device(px, py, z, c)).start()

    loop(1, 16, m_send)

    for d in (1, 2, 3):
        arrived(u_q.at[lax.rem(qb - d + 4, 4)], U_Q + d)
    u_o[qa] = (u_q[0] + u_q[1]) + (u_q[2] + u_q[3])
    for d in range(1, 8):
        to = lax.rem(qa + d, 8)
        remote(u_o.at[qa], u_o.at[qa], U_O + d, U_O + d, device(x, y, to * 4 + qb, c)).start()

    backward(near_pair, near_at, 4, 8)

    @pl.when(owner)
    def _():
        d_o[qa] = d_h[...]
        for d in range(1, 8):
            at = lax.rem(qa - d + 8, 8)
            arrived(d_o.at[at], D_O + at)
        d_g[x] = total8(d_o)

        def g_send(i):
            px, py = plane(i)
            remote(d_g.at[x], d_g.at[x], D_G + i, D_G + x, device(px, py, z, c)).start()

        loop(1, 16, g_send)

    def m_wait(i):
        px, py = plane(i)
        arrived(m_p.at[px * 4 + py], M_P + px * 4 + py)

    loop(1, 16, m_wait)
    m_q[qb] = jnp.sum(m_p[...], axis=0)
    for d in (1, 2, 3):
        to = lax.rem(qb + d, 4)
        remote(m_q.at[qb], m_q.at[qb], M_Q + d, M_Q + d, device(x, y, qa * 4 + to, c)).start()
    lay[...] = (lin[...] * scaling).astype(BF16)
    lay_copy = pltpu.make_async_copy(lay, lay_hbm, rs.at[OUT + 16])
    lay_copy.start()
    backward(far_pair, far_at, 0, 3)
    for d in (1, 2, 3):
        arrived(m_q.at[lax.rem(qb - d + 4, 4)], M_Q + d)
    m_o[qa] = (m_q[0] + m_q[1]) + (m_q[2] + m_q[3])
    for d in range(1, 8):
        to = lax.rem(qa + d, 8)
        remote(m_o.at[qa], m_o.at[qa], M_O + d, M_O + d, device(x, y, to * 4 + qb, c)).start()

    for d in range(1, 8):
        arrived(u_o.at[lax.rem(qa - d + 8, 8)], U_O + d)
    u_g[c, xy] = total8(u_o)

    def ug_send(i):
        px, py = plane(i)
        part = u_g.at[c, xy]
        remote(part, part, U_G + i, U_G + xy, device(px, py, z, c)).start()

    loop(1, 16, ug_send)

    backward(far_pair, far_at, 3, 8)

    def ug_wait(i):
        px, py = plane(i)
        arrived(u_g.at[c, px * 4 + py], U_G + px * 4 + py)

    loop(1, 16, ug_wait)
    ug_copy = remote(u_g.at[c], u_g.at[c], U_GC, U_GC, sib)
    ug_copy.start()

    def dg_wait(i):
        @pl.when(jnp.logical_or(i != x, jnp.logical_not(owner)))
        def _():
            arrived(d_g.at[i], D_G + i)

    loop(0, 4, dg_wait)
    dg_ref[...] = d_g[...].reshape(64, 128)
    ug_copy.wait()
    for k in range(2):
        for q in range(4):
            ug_ref[k * 32 : k * 32 + 32, q * 128 : q * 128 + 128] = u_g[
                k, q * 4 : q * 4 + 4
            ].reshape(32, 128)

    def sent(i):
        left_here(n_z.at[zl], N_Z + i)
        left_here(ap.at[c, x, zl], A_Z + i)
        left_here(d_p.at[0], D_P + i + 1)
        left_here(u_p.at[0], U_P + i + 1)
        left_here(m_p.at[xy], M_P + i + 1)
        left_here(u_g.at[c, xy], U_G + i + 1)

        @pl.when(owner)
        def _():
            left_here(d_g.at[x], D_G + i + 1)

    loop(0, 15, sent)
    for j in (0, 1, 2, 3, *range(5, 16)):
        left_here(w_piece, W_Z + j)
    for d in (1, 2, 3):
        left_here(ap.at[c, x], A_X + d)
        left_here(wn.at[c, y, x], W_X + d)
        left_here(wf.at[c, x, y], V_Y + d)
        left_here(d_s.at[0], D_Q + d)
        left_here(u_q.at[0], U_Q + d)
        left_here(m_q.at[0], M_Q + d)
    for hi in (0, 1):

        @pl.when(y + 4 * hi != qa)
        def _():
            left_here(d_h, D_O + hi)

    for d in range(1, 8):
        left_here(u_o.at[0], U_O + d)
        left_here(m_o.at[0], M_O + d)
    left_here(ap.at[c], A_CORE)
    block_sent(*near_y, W_PA, W_PB)
    block_sent(*far_x, V_PA, V_PB)
    lay_copy.wait()

    def stored(i):
        pltpu.make_async_copy(
            inp.at[:, columns(i)], inp_hbm.at[:, columns(i)], rs.at[OUT + i]
        ).wait()

    loop(0, 16, stored)

    for d in range(1, 8):
        arrived(m_o.at[lax.rem(qa - d + 8, 8)], M_O + d)
    mg_ref[...] = total8(m_o) / col_norm * factor


def hand_over(*refs):
    sources, targets, held, came, went = refs[:5], refs[5:10], refs[10:15], refs[15], refs[16]
    parts = []
    for i in (1, 0, 3, 4, 2):
        rows = sources[i].shape[0]
        step = 48 if i == 1 else rows
        for first in range(0, rows, step):
            at = pl.ds(first, step)
            parts.append((sources[i].at[at], held[i].at[at], targets[i].at[at]))
    into = [pltpu.make_async_copy(p[0], p[1], came.at[n]) for n, p in enumerate(parts)]
    out = [pltpu.make_async_copy(p[1], p[2], went.at[n]) for n, p in enumerate(parts)]
    for copy in into:
        copy.start()
    for first, second in zip(into, out):
        first.wait()
        second.start()
    for copy in out:
        copy.wait()


def body(tokens, base, down, up, magnitude, cotangent):
    anywhere = pl.BlockSpec(memory_space=pl.ANY)
    vmem = pl.BlockSpec(memory_space=pltpu.VMEM)
    shapes = (
        jax.ShapeDtypeStruct((TOK, UNITS), BF16),
        jax.ShapeDtypeStruct((TOK, FEAT), BF16),
        jax.ShapeDtypeStruct((1, UNITS), F32),
        jax.ShapeDtypeStruct((RANK, UNITS), F32),
        jax.ShapeDtypeStruct((RANK, 128), F32),
    )
    results = pl.pallas_call(
        kernel,
        out_shape=shapes,
        in_specs=[anywhere] * 6,
        out_specs=(anywhere, anywhere, vmem, vmem, vmem),
        scratch_shapes=[
            pltpu.VMEM((TOK, FEAT), BF16),
            pltpu.VMEM((128, UNITS), BF16),
            pltpu.VMEM((RANK, 128), BF16),
            pltpu.VMEM((RANK, UNITS), BF16),
            pltpu.VMEM((1, UNITS), F32),
            pltpu.VMEM((TOK, UNITS), BF16),
            pltpu.VMEM((2, 4, 4, 8, 32, 128), BF16),
            pltpu.VMEM((2, 4, 4, 8, 32, 128), BF16),
            pltpu.VMEM((2, 4, 16, 16, 128), BF16),
            pltpu.VMEM((2, 1, UNITS), F32),
            pltpu.VMEM((16, 1, UNITS), F32),
            pltpu.VMEM((TOK, UNITS), BF16),
            pltpu.VMEM((TOK, RANK), BF16),
            pltpu.VMEM((TOK, UNITS), F32),
            pltpu.VMEM((TOK, UNITS), BF16),
            pltpu.VMEM((TOK, FEAT), BF16),
            pltpu.VMEM((2, 4, 4, 4, 16, 128), F32),
            pltpu.VMEM((4, 4, 4, 16, 128), F32),
            pltpu.VMEM((4, 4, 4, 16, 128), BF16),
            pltpu.VMEM((16, 4, 16, 128), BF16),
            pltpu.VMEM((4, 16, 128), F32),
            pltpu.VMEM((4, 16, 128), F32),
            pltpu.VMEM((16, 128), F32),
            pltpu.VMEM((8, 16, 128), F32),
            pltpu.VMEM((4, 16, 128), F32),
            pltpu.VMEM((2, 4, 4, 8, 128), F32),
            pltpu.VMEM((4, 4, 8, 128), F32),
            pltpu.VMEM((4, 4, 8, 128), F32),
            pltpu.VMEM((16, 8, 128), F32),
            pltpu.VMEM((4, 8, 128), F32),
            pltpu.VMEM((8, 8, 128), F32),
            pltpu.VMEM((2, 16, 8, 128), F32),
            pltpu.VMEM((2, 1, UNITS), F32),
            pltpu.VMEM((16, 1, UNITS), F32),
            pltpu.VMEM((4, 1, UNITS), F32),
            pltpu.VMEM((8, 1, UNITS), F32),
            pltpu.SemaphoreType.DMA((TOTAL,)),
            pltpu.SemaphoreType.DMA((TOTAL,)),
        ],
        compiler_params=pltpu.CompilerParams(
            collective_id=0, has_side_effects=True, vmem_limit_bytes=60 * 1024 * 1024
        ),
    )(tokens, base, down.T, up, magnitude.reshape(1, UNITS), cotangent)
    lay, inp, mg, ug, dg = pl.pallas_call(
        hand_over,
        out_shape=shapes,
        in_specs=[anywhere] * 5,
        out_specs=(anywhere,) * 5,
        scratch_shapes=[pltpu.VMEM(shape.shape, shape.dtype) for shape in shapes]
        + [pltpu.SemaphoreType.DMA((8,)), pltpu.SemaphoreType.DMA((8,))],
        compiler_params=pltpu.CompilerParams(vmem_limit_bytes=60 * 1024 * 1024),
    )(*results)
    return lay, inp, mg.reshape(UNITS), ug, dg.T


def solution(mesh):
    placed = (
        P(("fsdp", "rep"), None),
        P("fsdp", None),
        P("fsdp", None),
        P(),
        P(),
        P(("fsdp", "rep"), None),
    )
    return jax.shard_map(
        body,
        mesh=mesh,
        in_specs=placed,
        out_specs=(P(("fsdp", "rep"), None), P(("fsdp", "rep"), None), P(), P(), P("fsdp", None)),
        check_vma=False,
    )
```
